512 devices in a mesh: dom: 128 (over z, x, core), narrow: 4 (over y).
Axes of the slice: x: 4, y: 4, z: 16, core: 2. Of those that a mesh axis runs over, the one named last changes fastest.
Arguments:
- state: float32 [13, 84, 131072], P(None, None, ('dom', 'narrow')), may hold values from -6 to 6
- predictor: float32 [13, 84, 131072], P(None, None, ('dom', 'narrow')), may hold values from -6 to 6
- degree: int32 [131072], P(('dom', 'narrow')), may hold values from 2 to 6
- material: int32 [131072], P(('dom', 'narrow')), may hold values from 0 to 31
- face_link: int32 [4, 131072], P(None, ('dom', 'narrow')), may hold values from 0 to 1407, as said below
- publish: int32 [4096], P(('dom', 'narrow')), may hold values from 0 to 255, as said below
- new_owner: int32 [131072], P(('dom', 'narrow')), may hold values from 0 to 127, as said below
- new_index: int32 [131072], P(('dom', 'narrow')), may hold values from 0 to 255, as said below
- derivative: float32 [3, 84, 84], replicated, may hold values from -0.625 to 0.625
- trace_ops: float32 [4, 28, 84], replicated, may hold values from -0.625 to 0.625
- lift_ops: float32 [4, 84, 28], replicated, may hold values from -0.5 to 0.5
- jacobians: float32 [32, 3, 13, 13], P('narrow'), may hold values from -1.75 to 1.75
- speeds: float32 [32], P('narrow'), may hold values from 0.5 to 3
- normals: float32 [3, 4, 131072], P(None, None, ('dom', 'narrow')), may hold values from -6 to 6
Outputs:
- corrected: float32 [13, 84, 131072], P(None, None, ('dom', 'narrow'))
- new_predictor: float32 [13, 84, 131072], P(None, None, ('dom', 'narrow'))
The draws below stay inside these ranges and needn't reach their ends.
Inputs may be any that keep to these rules, and one draw needn't show every extreme that they name: `face_link`: values below 1024 name face v // 256 of element v % 256 of the same block; each of the 384 entries of a block's remote table is named by exactly one face of that block. `publish`: the 8 entries of one block are distinct element numbers of that block. Elements keep their narrow index. At most 4 elements of one device have the same new_owner, and in every draw some device sends exactly 4 to one dom index; every device receives exactly 256 elements. The elements that arrive at one device have distinct new_index.
All inputs are finite; a program needn't handle non-finite values.
Results may differ from the reference program's by a relative error of at most 0.0003.
Values sent between devices are 32-bit elements; how exact they have to be, the bound alone decides.
No kernel may reach another device: no remote copies, remote signals or barrier semaphores. Data moves between devices by JAX's collectives and lax.ppermute only.
A program may use at most 128 MiB of HBM per device.

```python
import math
import jax
import jax.numpy as jnp
from jax import lax

FIELDS = 13
MODES = 84
FQ = 28
MATS = 32
EL = 256
PUBE = 8
ELEMS = 131072
N_DOM = 128
N_NARROW = 4


def migration_plan(key):
    blocks = N_DOM * N_NARROW
    share = EL // N_DOM
    key_level, key_shift, key_order, key_shuffle = jax.random.split(key, 4)
    levels = jax.random.randint(key_level, (N_NARROW, N_DOM), 0, share + 1)
    levels = levels.at[:, 0].set(share).at[:, 1].set(0)
    swing = levels - jnp.roll(levels, -1, axis=1)
    shifts = jax.random.randint(key_shift, (N_NARROW, 1, 1), 0, N_DOM)
    sources = jnp.arange(N_DOM, dtype=jnp.int32)[None, :, None]
    targets = jnp.arange(N_DOM, dtype=jnp.int32)[None, None, :]
    gap = (targets - sources + shifts) % N_DOM
    spread = jnp.broadcast_to(swing[:, None, :], (N_NARROW, N_DOM, N_DOM))
    counts = share + jnp.take_along_axis(spread, gap, axis=2)
    upper = jnp.cumsum(counts, axis=2)
    lower = upper - counts
    before = jnp.cumsum(counts, axis=1) - counts
    order_keys = jax.random.split(key_order, blocks)
    positions = jax.vmap(lambda one_key: jax.random.permutation(one_key, EL))(order_keys)
    positions = jnp.transpose(positions.reshape(N_DOM, N_NARROW, EL), (1, 0, 2)).astype(jnp.int32)
    dest = jnp.sum((positions[:, :, :, None] >= upper[:, :, None, :]).astype(jnp.int32), axis=3)
    pair_rank = positions - jnp.take_along_axis(lower, dest, axis=2)
    raw_index = jnp.take_along_axis(before, dest, axis=2) + pair_rank
    shuffle_keys = jax.random.split(key_shuffle, blocks)
    shuffles = jax.vmap(lambda one_key: jax.random.permutation(one_key, EL))(shuffle_keys).reshape(N_NARROW, N_DOM, EL).astype(jnp.int32)
    narrow_ids = jnp.arange(N_NARROW, dtype=jnp.int32)[:, None, None]
    flat_shuffle = shuffles.reshape(-1)
    new_slot = flat_shuffle[(narrow_ids * N_DOM + dest) * EL + raw_index]
    owner_out = jnp.transpose(dest, (1, 0, 2)).reshape(-1).astype(jnp.int32)
    index_out = jnp.transpose(new_slot, (1, 0, 2)).reshape(-1).astype(jnp.int32)
    return (owner_out, index_out)


def draw_new_owner(key, part):
    return migration_plan(key)[0]


def draw_new_index(key, part):
    return migration_plan(key)[1]


def draw_face_link(key, part):
    key = jax.random.fold_in(key, 11)
    blocks = N_DOM * N_NARROW
    remote_cols = 12 * N_NARROW * PUBE
    key_order, key_near = jax.random.split(key, 2)
    order_keys = jax.random.split(key_order, blocks)
    near_keys = jax.random.split(key_near, blocks)

    def one_block(order_key, near_key):
        placing = jax.random.permutation(order_key, 4 * EL).astype(jnp.int32)
        near_link = jax.random.randint(near_key, (4 * EL,), 0, 4 * EL).astype(jnp.int32)
        return jnp.where(placing < remote_cols, 4 * EL + placing, near_link).reshape(4, EL)
    links = jax.vmap(one_block)(order_keys, near_keys)
    return jnp.transpose(links, (1, 0, 2)).reshape(4, ELEMS).astype(jnp.int32)


def draw_publish(key, part):
    key = jax.random.fold_in(key, 12)
    block_keys = jax.random.split(key, N_DOM * N_NARROW)
    chosen = jax.vmap(lambda one_key: jax.random.permutation(one_key, EL)[:PUBE])(block_keys)
    return chosen.reshape(-1).astype(jnp.int32)


def with_ends(drawn, own_key, smallest, largest):
    index_at = [jax.random.randint(jax.random.fold_in(own_key, axis), (), 0, length) for axis, length in enumerate(drawn.shape)]
    longest = drawn.shape.index(max(drawn.shape))
    next_to = index_at[:longest] + [(index_at[longest] + 1) % drawn.shape[longest]] + index_at[longest + 1:]
    return drawn.at[tuple(index_at)].set(smallest).at[tuple(next_to)].set(largest)


def steps_of(own_key, extent, shards, least, top_value):
    gain = 1.0
    for position, shards_of in shards:
        steps = jax.random.uniform(jax.random.fold_in(jax.random.fold_in(own_key, 6), position), (shards_of,), jnp.float32, least / len(shards), top_value / len(shards))
        gain = gain * jnp.repeat(jnp.exp(steps), extent[position] // shards_of).reshape((-1,) + (1,) * (len(extent) - 1 - position))
    return gain


def bell_draw(own_key, shape, scale, reach, shards=(), kind=jnp.bfloat16):
    entries = jax.random.normal(own_key, shape, jnp.float32) * scale
    if len(shards) > 0:
        entries = steps_of(own_key, shape, shards, -0.22, 0.18) * entries
    return jnp.clip(entries, min=-reach, max=reach).astype(kind)


def setup_inputs(seed: int = 0) -> dict:
    splits = jax.random.split(jax.random.key(seed), 15)
    return {
        "state": bell_draw(splits[0], (FIELDS, MODES, ELEMS), 1.0, 6.0, ((2, 512),), jnp.float32),
        "predictor": bell_draw(splits[1], (FIELDS, MODES, ELEMS), 1.0, 6.0, ((2, 512),), jnp.float32),
        "degree": with_ends(jax.random.randint(splits[2], (ELEMS,), 2, 7), jax.random.fold_in(splits[2], 1), 2, 6).astype(jnp.int32),
        "material": with_ends(jax.random.randint(splits[3], (ELEMS,), 0, MATS), jax.random.fold_in(splits[3], 1), 0, MATS - 1).astype(jnp.int32),
        "face_link": draw_face_link(jax.random.fold_in(splits[14], 71), 0),
        "publish": draw_publish(jax.random.fold_in(splits[14], 71), 0),
        "new_owner": draw_new_owner(jax.random.fold_in(splits[14], 71), 0),
        "new_index": draw_new_index(jax.random.fold_in(splits[14], 71), 0),
        "derivative": bell_draw(splits[8], (3, MODES, MODES), MODES ** -0.5, 0.625, (), jnp.float32),
        "trace_ops": bell_draw(splits[9], (4, FQ, MODES), MODES ** -0.5, 0.625, (), jnp.float32),
        "lift_ops": bell_draw(splits[10], (4, MODES, FQ), (4 * FQ) ** -0.5, 0.5, (), jnp.float32),
        "jacobians": bell_draw(splits[11], (MATS, 3, FIELDS, FIELDS), FIELDS ** -0.5, 1.75, ((0, 4),), jnp.float32),
        "speeds": jnp.clip(jnp.exp(math.log(3.0) - 1.7917595 * jax.random.uniform(splits[12], (MATS,), jnp.float32) ** steps_of(splits[12], (MATS,), ((0, 4),), -0.2, 0.2)), 0.5, 3.0),
        "normals": bell_draw(splits[13], (3, 4, ELEMS), 1.0, 6.0, ((2, 512),), jnp.float32),
    }


highest = lax.Precision.HIGHEST
time_step = 1.5


def mode_degree(count):
    indices = jnp.arange(count, dtype=jnp.int32)
    degrees = jnp.zeros((count,), jnp.int32)
    for step_order in range(1, 7):
        threshold = step_order * (step_order + 1) * (step_order + 2) // 6
        degrees = degrees + (indices >= threshold).astype(jnp.int32)
    return degrees


def mode_mask(degree_row, count):
    return (mode_degree(count)[:, None] <= degree_row[None, :]).astype(jnp.float32)


def element_jacobian(jac_table, material_row):
    return jnp.transpose(jnp.take(jac_table, material_row, axis=0), (1, 2, 3, 0))


def spatial(field_data, derivative, jacobian):
    slopes = jnp.einsum('dmk,fke->dfme', derivative, field_data, precision=highest)
    total = jnp.zeros(field_data.shape, jnp.float32)
    for direction in range(3):
        for source in range(field_data.shape[0]):
            total = total + jacobian[direction, :, source, None, :] * slopes[direction, source][None]
    return total


def flux_of(normal_blk, jacobian, own_trace, outside, wave_speed):
    directed = normal_blk[0][:, None, None, :] * jacobian[0][None]
    for direction in range(1, 3):
        directed = directed + normal_blk[direction][:, None, None, :] * jacobian[direction][None]
    summed = own_trace + outside
    result = 0.5 * wave_speed * (own_trace - outside)
    for source in range(own_trace.shape[0]):
        result = result + 0.5 * jnp.transpose(directed[:, :, source, :], (1, 0, 2))[:, None, :, :] * summed[source][None]
    return result


def predict_block(field_data, degree_row, material_row, derivative, jac_table):
    kept = mode_mask(degree_row, field_data.shape[1])
    jacobian = element_jacobian(jac_table, material_row)
    derivative_term = field_data
    integral = time_step * field_data
    factor = time_step
    for time_order in range(1, 7):
        derivative_term = -spatial(derivative_term, derivative, jacobian) * kept[None]
        factor = factor * time_step / (time_order + 1)
        active = (degree_row >= time_order).astype(jnp.float32)
        integral = integral + (factor * active)[None, None, :] * derivative_term
    return integral


def reference(state, predictor, degree, material, face_link, publish, new_owner, new_index, derivative, trace_ops, lift_ops, jacobians, speeds, normals):
    blocks = N_DOM * N_NARROW
    fields, mode_count, elem_total = state.shape
    points = trace_ops.shape[1]
    block_ids = jnp.arange(blocks, dtype=jnp.int32)

    def block_cut(array, block):
        return lax.dynamic_slice_in_dim(array, (block * EL).astype(jnp.int32), EL, array.ndim - 1)

    def publish_block(block):
        degree_blk = block_cut(degree, block)
        pred_blk = block_cut(predictor, block) * mode_mask(degree_blk, mode_count)[None]
        chosen = lax.dynamic_slice_in_dim(publish, (block * PUBE).astype(jnp.int32), PUBE, 0)
        picked = jnp.take(pred_blk, chosen, axis=2)
        traces = jnp.einsum('aqm,fmj->fqaj', trace_ops, picked, precision=highest)
        return traces.reshape(fields, points, 4 * PUBE)

    published = lax.map(publish_block, block_ids)

    def correct_one(block):
        dom_index = block // N_NARROW
        nearby_ids = []
        for side_step in (-1, 0, 1):
            for sibling in range(N_NARROW):
                nearby_ids.append(((dom_index + side_step) % N_DOM) * N_NARROW + sibling)
        neighbours = jnp.stack(nearby_ids).astype(jnp.int32)
        remote = jnp.take(published, neighbours, axis=0)
        remote = jnp.moveaxis(remote, 0, 2).reshape(fields, points, -1)
        degree_blk = block_cut(degree, block)
        material_blk = block_cut(material, block)
        kept = mode_mask(degree_blk, mode_count)
        pred_kept = block_cut(predictor, block) * kept[None]
        jacobian = element_jacobian(jacobians, material_blk)
        wave_speed = jnp.take(speeds, material_blk, axis=0)
        own_trace = jnp.einsum('aqm,fme->fqae', trace_ops, pred_kept, precision=highest)
        trace_table = jnp.concatenate([own_trace.reshape(fields, points, 4 * EL), remote], axis=2)
        links = block_cut(face_link, block)
        outside = jnp.take(trace_table, links.reshape(-1), axis=2).reshape(own_trace.shape)
        face_flux = flux_of(block_cut(normals, block), jacobian, own_trace, outside, wave_speed)
        lifted = jnp.einsum('amq,fqae->fme', lift_ops, face_flux, precision=highest)
        return (block_cut(state, block) - spatial(pred_kept, derivative, jacobian) - lifted) * kept[None]

    updated_blocks = lax.map(correct_one, block_ids)
    updated = jnp.moveaxis(updated_blocks, 0, 2).reshape(fields, mode_count, elem_total)
    positions = jnp.arange(elem_total, dtype=jnp.int32)
    sibling_index = (positions // EL) % N_NARROW
    target = (new_owner * N_NARROW + sibling_index) * EL + new_index
    corrected = jnp.zeros_like(updated).at[:, :, target].set(updated)
    degree_new = jnp.zeros_like(degree).at[target].set(degree)
    material_new = jnp.zeros_like(material).at[target].set(material)

    def predict_one(block):
        return predict_block(block_cut(corrected, block), block_cut(degree_new, block), block_cut(material_new, block), derivative, jacobians)

    ahead_blocks = lax.map(predict_one, block_ids)
    new_predictor = jnp.moveaxis(ahead_blocks, 0, 2).reshape(fields, mode_count, elem_total)
    return corrected, new_predictor
```

```python
import functools
import jax
import jax.numpy as jnp
from jax import lax
from jax.experimental import pallas as pl
from jax.experimental.pallas import tpu as pltpu
from jax.sharding import PartitionSpec as P

time_step = 1.5
F = 13
M = 84
MS = 88
MP = 96
E = 256
QP = 32
AR = 176
SLOTS = 512
PAY = 1152
INFO = F * MS
PICK = F * 128
JROWS = 640
f32, bf16 = jnp.float32, jnp.bfloat16


def split(x):
    hi = x.astype(bf16)
    return hi, (x - hi.astype(f32)).astype(bf16)


def dot(a, b, contract=((1,), (0,))):
    return lax.dot_general(a, b, (contract, ((), ())), preferred_element_type=f32)


NT = ((1,), (1,))


def mode_rows(count):
    m = lax.broadcasted_iota(jnp.int32, (count, E), 0)
    deg = jnp.zeros((count, E), jnp.int32)
    for p in range(1, 7):
        deg = deg + (m >= p * (p + 1) * (p + 2) // 6).astype(jnp.int32)
    return jnp.where(m < M, deg, 99)


def keep_rows(degree_row, count):
    return (mode_rows(count) <= degree_row).astype(f32)


def pad_rows(x, rows):
    return jnp.concatenate([x, jnp.zeros((rows - x.shape[0], x.shape[1]), x.dtype)], axis=0)


def load_derivative(der_ref, scr):
    scr[...] = jnp.zeros(scr.shape, f32)
    for d in range(3):
        scr[d * MS : d * MS + M, 0:M] = der_ref[d]
    hi, lo = split(scr[:, 0:M])
    hi, lo = hi.astype(f32), lo.astype(f32)
    return jnp.concatenate([hi, hi, lo], axis=1).astype(bf16)


def slopes_into(x_ref, matrices, s_ref):
    for f in range(F):
        hi, lo = split(x_ref[f, 0:M, :])
        hi, lo = hi.astype(f32), lo.astype(f32)
        s_ref[f] = dot(matrices, jnp.concatenate([hi, lo, hi], axis=0).astype(bf16))


def apply_jacobian(s_ref, a_ref, half, blocks, finish):
    lanes = pl.ds(half * 128, 128)

    def body(i, carry):
        r = pl.multiple_of(i * 16, 16)
        acc = [[None] * F for _ in range(2)]
        for d in range(3):
            for f in range(F):
                x = [s_ref[f, pl.ds(d * MS + r + 8 * t, 8), lanes] for t in range(2)]
                for g in range(F):
                    w = jnp.broadcast_to(a_ref[pl.ds(d * AR + g * F + f, 1), lanes], (8, 128))
                    for t in range(2):
                        acc[t][g] = w * x[t] if acc[t][g] is None else acc[t][g] + w * x[t]
        for t in range(2):
            finish(pl.multiple_of(r + 8 * t, 8), lanes, acc[t])
        return carry

    lax.fori_loop(0, blocks, body, 0)


def material_matrix(jac_ref, onehot):
    table = jac_ref[...]
    hi = table.astype(bf16)
    rest = table - hi.astype(f32)
    mid, lo = split(rest)
    tn = ((0,), (0,))
    return dot(hi, onehot, tn) + dot(mid, onehot, tn) + dot(lo, onehot, tn)


def material_onehot(material_row, me):
    k = lax.broadcasted_iota(jnp.int32, (32, E), 0)
    ident = lax.rem(me - k // 8 + 4, 4) * 8 + k % 8
    return (ident == material_row).astype(f32).astype(bf16)


def pick_kernel(pred_ref, degree_ref, publish_ref, jac_ref, speed_ref, out_ref):
    keep = keep_rows(degree_ref[...], M)
    e = lax.broadcasted_iota(jnp.int32, (16, E), 1)
    onehot = (e == publish_ref[...]).astype(f32).astype(bf16)
    out_ref[...] = jnp.zeros(out_ref.shape, f32)
    for f in range(F):
        hi, lo = split(pred_ref[f] * keep)
        picked = dot(onehot, hi, NT) + dot(onehot, lo, NT)
        out_ref[:, f * 128 : f * 128 + M] = picked[0:8]
    for d in range(3):
        for g in range(F):
            at = PICK + d * AR + g * F
            out_ref[:, at : at + F] = jac_ref[d, g]
    out_ref[:, PICK + 3 * AR : PICK + 3 * AR + 1] = speed_ref[...]


def trace_matrix(trace_ref, scr):
    scr[...] = jnp.zeros(scr.shape, f32)
    for a in range(4):
        scr[a * QP : a * QP + 28, 0:M] = trace_ref[a]
    return split(scr[...])


def link_place(link, me):
    w = link - 4 * E
    block, a, j = w // 32, (w // 8) % 4, w % 8
    step = lax.rem(me - block % 4 + 4, 4)
    far = 4 * E + a * 128 + (block // 4) * 32 + step * 8 + j
    return jnp.where(link < 4 * E, link, far)


def trace_kernel(pred_ref, degree_ref, trace_ref, link_ref, own_ref, near_ref, tscr, both):
    keep = keep_rows(degree_ref[...], MP)
    thi, tlo = trace_matrix(trace_ref, tscr)
    thi, tlo = thi[:, 0:MP], tlo[:, 0:MP]
    thh = jnp.concatenate([thi, thi], axis=1)
    for f in range(F):
        x = pad_rows(pred_ref[f], MP) * keep
        hi, lo = split(x)
        t = dot(thh, jnp.concatenate([hi, lo], axis=0)) + dot(tlo, hi)
        for a in range(4):
            own_ref[a, f * QP : (f + 1) * QP, :] = t[a * QP : (a + 1) * QP]
    for a in range(4):
        hi, lo = split(own_ref[a])
        both[0 : F * QP, a * E : (a + 1) * E] = hi
        both[F * QP :, a * E : (a + 1) * E] = lo
    k = lax.broadcasted_iota(jnp.int32, (4 * E, E), 0)
    for a in range(4):
        onehot = (k == link_ref[a : a + 1, :]).astype(f32).astype(bf16)
        r = dot(both[...], onehot)
        near_ref[a] = r[0 : F * QP] + r[F * QP :]


def local_kernel(me_ref, state_ref, pred_ref, degree_ref, material_ref, jac_ref, der_ref, base_ref, a_ref, x, s, dscr):
    keep = keep_rows(degree_ref[...], MP)
    for f in range(F):
        x[f] = pad_rows(pred_ref[f], MP) * keep
    a_ref[...] = material_matrix(jac_ref, material_onehot(material_ref[...], me_ref[0]))
    slopes_into(x, load_derivative(der_ref, dscr), s)
    for f in range(F):
        base_ref[f] = pad_rows(state_ref[f], MP)

    def finish(r, lanes, acc):
        for g in range(F):
            base_ref[g, pl.ds(r, 8), lanes] = base_ref[g, pl.ds(r, 8), lanes] - acc[g]

    for half in range(2):
        apply_jacobian(s, a_ref, half, MP // 16, finish)


def flux_kernel(
    me_ref, own_ref, near_ref, base_ref, a_ref, pick_ref, link_ref, normals_ref, trace_ref, lift_ref, degree_ref, material_ref,
    owner_row_ref, owner_col_ref, index_ref, out_ref, tscr, far, outside, lscr, dirs, flux, u,
):
    me = me_ref[0]
    thi, tlo = trace_matrix(trace_ref, tscr)
    for f in range(F):
        phi, plo = split(pick_ref[:, f * 128 : (f + 1) * 128])
        t = dot(thi, phi, NT) + dot(thi, plo, NT) + dot(tlo, phi, NT)
        for a in range(4):
            far[f * QP : (f + 1) * QP, a * 128 : (a + 1) * 128] = t[a * QP : (a + 1) * QP]
    fhi, flo = split(far[...])
    both = jnp.concatenate([fhi, flo], axis=0)
    k = lax.broadcasted_iota(jnp.int32, (4 * 128, E), 0) + 4 * E
    for a in range(4):
        onehot = (k == link_place(link_ref[a : a + 1, :], me)).astype(f32).astype(bf16)
        r = dot(both, onehot)
        outside[a] = near_ref[a] + r[0 : F * QP] + r[F * QP :]
    speed = a_ref[3 * AR : 3 * AR + 1, :] * 0.5
    for a in range(4):
        total = normals_ref[0, a : a + 1, :] * a_ref[0:AR]
        for d in range(1, 3):
            total = total + normals_ref[d, a : a + 1, :] * a_ref[d * AR : (d + 1) * AR]
        dirs[a] = 0.5 * total

    def face(i, carry):
        a, lanes = i // 2, pl.ds(pl.multiple_of((i % 2) * 128, 128), 128)
        sp = a_ref[3 * AR : 3 * AR + 1, lanes] * 0.5
        for f0, f1 in ((0, 5), (5, 9), (9, 13)):
            acc = {}
            for f in range(f0, f1):
                for t in range(4):
                    rows = pl.ds(f * QP + t * 8, 8)
                    acc[f, t] = sp * (own_ref[a, rows, lanes] - outside[a, rows, lanes])
            for g in range(F):
                both_sides = [own_ref[a, pl.ds(g * QP + t * 8, 8), lanes] + outside[a, pl.ds(g * QP + t * 8, 8), lanes] for t in range(4)]
                for f in range(f0, f1):
                    w = jnp.broadcast_to(dirs[a, pl.ds(f * F + g, 1), lanes], (8, 128))
                    for t in range(4):
                        acc[f, t] = acc[f, t] + w * both_sides[t]
            for f in range(f0, f1):
                for t in range(4):
                    flux[f, pl.ds(a * QP + t * 8, 8), lanes] = acc[f, t]
        return carry

    lax.fori_loop(0, 8, face, 0)
    lscr[...] = jnp.zeros(lscr.shape, f32)
    for a in range(4):
        lscr[0:M, a * QP : a * QP + 28] = lift_ref[a]
    lhi, llo = split(lscr[...])
    lhh = jnp.concatenate([lhi, lhi], axis=1)
    keep = keep_rows(degree_ref[...], MS)
    for f in range(F):
        hi, lo = split(flux[f])
        lifted = dot(lhh, jnp.concatenate([hi, lo], axis=0)) + dot(llo, hi)
        u[f * MS : (f + 1) * MS, :] = (base_ref[f, 0:MS, :] - lifted[0:MS]) * keep
    u[INFO : INFO + 8, :] = jnp.concatenate(
        [degree_ref[...], material_ref[...], index_ref[...] + 1, jnp.zeros((5, E), jnp.int32)], axis=0
    ).astype(f32)
    owner = owner_row_ref[...]
    before = lax.broadcasted_iota(jnp.int32, (E, E), 0) < lax.broadcasted_iota(jnp.int32, (E, E), 1)
    rank = jnp.sum(jnp.where((owner_col_ref[...] == owner) & before, 1.0, 0.0), axis=0, keepdims=True)
    slot = owner * 4 + rank.astype(jnp.int32)
    pick = (lax.broadcasted_iota(jnp.int32, (SLOTS, E), 0) == slot).astype(f32).astype(bf16)
    for c in range(3):
        hi, lo = split(u[c * 384 : (c + 1) * 384, :])
        out_ref[:, :, c * 384 : (c + 1) * 384] = (dot(pick, hi, NT) + dot(pick, lo, NT)).reshape(SLOTS // 4, 4, 384)


def predict_kernel(me_ref, arrived_ref, jac_ref, der_ref, corrected_ref, ahead_ref, c, r, x, s, a, dscr, keep, ahead):
    arrived = arrived_ref[...].reshape(SLOTS, PAY)
    info = jnp.transpose(arrived[:, PAY - 128 :])
    lead = info[INFO - (PAY - 128) : INFO - (PAY - 128) + 1]
    slot_row = lax.broadcasted_iota(jnp.int32, (SLOTS, SLOTS), 1)
    slot_col = lax.broadcasted_iota(jnp.int32, (SLOTS, SLOTS), 0)
    degree_col = arrived[:, INFO : INFO + 1]
    ahead_of = (degree_col > lead) | ((degree_col == lead) & (slot_col < slot_row))
    rank = jnp.sum(jnp.where(ahead_of, 1.0, 0.0), axis=0, keepdims=True)
    rank = jnp.where(lead > 0, rank, -1.0).astype(jnp.int32)
    pick = (lax.broadcasted_iota(jnp.int32, (E, SLOTS), 0) == rank).astype(f32).astype(bf16)
    for i in range(3):
        hi, lo = split(arrived[:, i * 384 : (i + 1) * 384])
        r[:, i * 384 : (i + 1) * 384] = dot(pick, hi) + dot(pick, lo)
        c[i * 384 : (i + 1) * 384, :] = jnp.transpose(r[:, i * 384 : (i + 1) * 384])
    place = r[:, INFO + 2 : INFO + 3].astype(jnp.int32)
    spread = (lax.broadcasted_iota(jnp.int32, (E, E), 1) + 1 == place).astype(f32).astype(bf16)
    degree = c[INFO : INFO + 1, :].astype(jnp.int32)
    material = c[INFO + 1 : INFO + 2, :].astype(jnp.int32)
    a[...] = material_matrix(jac_ref, material_onehot(material, me_ref[0]))
    keep[...] = keep_rows(degree, MP)
    matrices = load_derivative(der_ref, dscr)
    for f in range(F):
        rows = c[f * MS : (f + 1) * MS, :]
        hi, lo = split(rows)
        corrected_ref[f] = (dot(hi, spread) + dot(lo, spread))[0:M]
        x[f] = pad_rows(rows, MP)
        ahead[f] = time_step * pad_rows(rows, MP)
    top = [jnp.max(degree[:, 128 * half : 128 * (half + 1)]) for half in range(2)]
    blocks = [jnp.where(t <= 2, 1, jnp.where(t == 3, 2, jnp.where(t == 4, 3, jnp.where(t == 5, 4, 6)))) for t in top]

    def step(j, factor):
        factor = factor * time_step / (j + 1).astype(f32)
        slopes_into(x, matrices, s)
        active = jnp.where(degree >= j, factor, 0.0)
        for half in range(2):
            weight = active[:, 128 * half : 128 * (half + 1)]

            def finish(at, lanes, acc):
                kept = -keep[pl.ds(at, 8), lanes]
                for g in range(F):
                    t = acc[g] * kept
                    x[g, pl.ds(at, 8), lanes] = t
                    ahead[g, pl.ds(at, 8), lanes] = ahead[g, pl.ds(at, 8), lanes] + weight * t

            apply_jacobian(s, a, half, jnp.where(j <= top[half], blocks[half], 0), finish)
        return factor

    lax.fori_loop(1, 7, step, jnp.float32(time_step))
    for f in range(F):
        hi, lo = split(ahead[f])
        ahead_ref[f] = (dot(hi, spread) + dot(lo, spread))[0:M]


def call(kernel, outs, scratch, smem, args, flops, limit=24):
    specs = [pl.BlockSpec(memory_space=pltpu.SMEM if i < smem else pltpu.VMEM) for i in range(len(args))]
    return pl.pallas_call(
        kernel,
        out_shape=[jax.ShapeDtypeStruct(o, f32) for o in outs],
        in_specs=specs,
        out_specs=[pl.BlockSpec(memory_space=pltpu.VMEM) for _ in outs],
        scratch_shapes=[pltpu.VMEM(shape, kind) for shape, kind in scratch],
        compiler_params=pltpu.CompilerParams(vmem_limit_bytes=limit * 1024 * 1024),
        cost_estimate=pl.CostEstimate(flops=flops, bytes_accessed=4000000, transcendentals=0),
    )(*args)


def ring(count, step):
    return [(i, (i + step) % count) for i in range(count)]


def shards(
    state, predictor, degree, material, face_link, publish, new_owner, new_index, derivative, trace_ops, lift_ops,
    jacobians, speeds, normals,
):
    me = lax.axis_index("narrow").astype(jnp.int32).reshape(1)
    row = lambda v: v.reshape(1, E)
    published = jnp.concatenate([publish, jnp.full((8,), -1, jnp.int32)]).reshape(16, 1)
    (mine,) = call(pick_kernel, [(8, PICK + JROWS)], [], 0, [predictor, row(degree), published, jnp.transpose(jacobians, (1, 2, 0, 3)), speeds.reshape(8, 1)], 10**9)
    shared = jnp.concatenate([mine] + [lax.ppermute(mine, "narrow", ring(4, s)) for s in (1, 2, 3)], axis=0)
    picks, jac = shared[:, :PICK], shared[:, PICK:]
    low = lax.ppermute(picks, "dom", ring(128, 1))
    high = lax.ppermute(picks, "dom", ring(128, -1))
    own, near = call(
        trace_kernel,
        [(4, F * QP, E), (4, F * QP, E)],
        [((128, 128), f32), ((2 * F * QP, 4 * E), bf16)],
        0,
        [predictor, row(degree), trace_ops, face_link],
        4 * 10**9,
    )
    base, a = call(
        local_kernel,
        [(F, MP, E), (JROWS, E)],
        [((F, MP, E), f32), ((F, 272, E), f32), ((272, 128), f32)],
        1,
        [me, state, predictor, row(degree), row(material), jac, derivative],
        4 * 10**9,
    )
    around = jnp.concatenate([low, picks, high, jnp.zeros((32, PICK), f32)], axis=0)
    (outgoing,) = call(
        flux_kernel,
        [(128, 4, PAY)],
        [
            ((128, 128), f32),
            ((F * QP, 512), f32),
            ((4, F * QP, E), f32),
            ((96, 128), f32),
            ((4, AR, E), f32),
            ((F, 128, E), f32),
            ((PAY, E), f32),
        ],
        1,
        [me, own, near, base, a, around, face_link, normals, trace_ops, lift_ops, row(degree), row(material),
         row(new_owner), new_owner.reshape(E, 1), row(new_index)],
        4 * 10**9,
    )
    arrived = lax.all_to_all(outgoing, "dom", split_axis=0, concat_axis=0, tiled=True)
    corrected, ahead = call(
        predict_kernel,
        [(F, M, E), (F, M, E)],
        [
            ((PAY, E), f32),
            ((E, PAY), f32),
            ((F, MP, E), f32),
            ((F, 272, E), f32),
            ((JROWS, E), f32),
            ((272, 128), f32),
            ((MP, E), f32),
            ((F, MP, E), f32),
        ],
        1,
        [me, arrived, jac, derivative],
        10**10,
    )
    return corrected, ahead


def solution(mesh):
    both = ("dom", "narrow")
    placed = (
        P(None, None, both), P(None, None, both), P(both), P(both), P(None, both), P(both), P(both), P(both),
        P(), P(), P(), P("narrow", None, None, None), P("narrow"), P(None, None, both),
    )
    return jax.shard_map(
        shards,
        mesh=mesh,
        in_specs=placed,
        out_specs=(P(None, None, both), P(None, None, both)),
        check_vma=False,
    )
```

```python
import functools
import jax
import jax.numpy as jnp
from jax import lax
from jax.experimental import pallas as pl
from jax.experimental.pallas import tpu as pltpu
from jax.sharding import PartitionSpec as P

time_step = 1.5
F = 13
M = 84
MS = 88
MP = 96
E = 256
QP = 32
AR = 176
SLOTS = 512
PAY = 1152
FORWARD = 64
INFO = F * MS
PICK = F * 128
JROWS = 640
f32, bf16 = jnp.float32, jnp.bfloat16


def split(x):
    hi = x.astype(bf16)
    return hi, (x - hi.astype(f32)).astype(bf16)


def dot(a, b, contract=((1,), (0,))):
    return lax.dot_general(a, b, (contract, ((), ())), preferred_element_type=f32)


NT = ((1,), (1,))


def mode_rows(count):
    m = lax.broadcasted_iota(jnp.int32, (count, E), 0)
    deg = jnp.zeros((count, E), jnp.int32)
    for p in range(1, 7):
        deg = deg + (m >= p * (p + 1) * (p + 2) // 6).astype(jnp.int32)
    return jnp.where(m < M, deg, 99)


def keep_rows(degree_row, count):
    return (mode_rows(count) <= degree_row).astype(f32)


def pad_rows(x, rows):
    return jnp.concatenate([x, jnp.zeros((rows - x.shape[0], x.shape[1]), x.dtype)], axis=0)


def load_derivative(der_ref, scr):
    scr[...] = jnp.zeros(scr.shape, f32)
    for d in range(3):
        scr[d * MS : d * MS + M, 0:M] = der_ref[d]
    hi, lo = split(scr[:, 0:M])
    hi, lo = hi.astype(f32), lo.astype(f32)
    return jnp.concatenate([hi, hi, lo], axis=1).astype(bf16)


def slopes_into(x_ref, matrices, s_ref):
    for f in range(F):
        hi, lo = split(x_ref[f, 0:M, :])
        hi, lo = hi.astype(f32), lo.astype(f32)
        s_ref[f] = dot(matrices, jnp.concatenate([hi, lo, hi], axis=0).astype(bf16))


def apply_jacobian(s_ref, a_ref, half, blocks, finish):
    lanes = pl.ds(half * 128, 128)

    def body(i, carry):
        r = pl.multiple_of(i * 16, 16)
        acc = [[None] * F for _ in range(2)]
        for d in range(3):
            for f in range(F):
                x = [s_ref[f, pl.ds(d * MS + r + 8 * t, 8), lanes] for t in range(2)]
                for g in range(F):
                    w = jnp.broadcast_to(a_ref[pl.ds(d * AR + g * F + f, 1), lanes], (8, 128))
                    for t in range(2):
                        acc[t][g] = w * x[t] if acc[t][g] is None else acc[t][g] + w * x[t]
        for t in range(2):
            finish(pl.multiple_of(r + 8 * t, 8), lanes, acc[t])
        return carry

    lax.fori_loop(0, blocks, body, 0)


def material_matrix(jac_ref, onehot):
    table = jac_ref[...]
    hi = table.astype(bf16)
    rest = table - hi.astype(f32)
    mid, lo = split(rest)
    tn = ((0,), (0,))
    return dot(hi, onehot, tn) + dot(mid, onehot, tn) + dot(lo, onehot, tn)


def material_onehot(material_row, me):
    k = lax.broadcasted_iota(jnp.int32, (32, E), 0)
    ident = lax.rem(me - k // 8 + 4, 4) * 8 + k % 8
    return (ident == material_row).astype(f32).astype(bf16)


def pick_kernel(pred_ref, degree_ref, publish_ref, jac_ref, speed_ref, out_ref):
    keep = keep_rows(degree_ref[...], M)
    eye = lax.broadcasted_iota(jnp.int32, (8, 8), 0) == lax.broadcasted_iota(jnp.int32, (8, 8), 1)
    column = lambda v: jnp.sum(jnp.where(eye, v, 0.0), axis=1, keepdims=True)
    published = pad_rows(column(publish_ref[...].astype(f32)), 16).astype(jnp.int32)
    e = lax.broadcasted_iota(jnp.int32, (16, E), 1)
    onehot = (e == published).astype(f32).astype(bf16)
    out_ref[...] = jnp.zeros(out_ref.shape, f32)
    for f in range(F):
        hi, lo = split(pred_ref[f] * keep)
        picked = dot(onehot, hi, NT) + dot(onehot, lo, NT)
        out_ref[:, f * 128 : f * 128 + M] = picked[0:8]
    for d in range(3):
        for g in range(F):
            at = PICK + d * AR + g * F
            out_ref[:, at : at + F] = jac_ref[d, g]
    out_ref[:, PICK + 3 * AR : PICK + 3 * AR + 1] = column(speed_ref[...])


def trace_matrix(trace_ref, scr):
    scr[...] = jnp.zeros(scr.shape, f32)
    for a in range(4):
        scr[a * QP : a * QP + 28, 0:M] = trace_ref[a]
    return split(scr[...])


def link_place(link, me):
    w = link - 4 * E
    block, a, j = w // 32, (w // 8) % 4, w % 8
    step = lax.rem(me - block % 4 + 4, 4)
    far = 4 * E + a * 128 + (block // 4) * 32 + step * 8 + j
    return jnp.where(link < 4 * E, link, far)


def trace_kernel(pred_ref, degree_ref, trace_ref, link_ref, own_ref, near_ref, tscr, both):
    keep = keep_rows(degree_ref[...], MP)
    thi, tlo = trace_matrix(trace_ref, tscr)
    thi, tlo = thi[:, 0:MP], tlo[:, 0:MP]
    thh = jnp.concatenate([thi, thi], axis=1)
    for f in range(F):
        x = pad_rows(pred_ref[f], MP) * keep
        hi, lo = split(x)
        t = dot(thh, jnp.concatenate([hi, lo], axis=0)) + dot(tlo, hi)
        for a in range(4):
            own_ref[a, f * QP : (f + 1) * QP, :] = t[a * QP : (a + 1) * QP]
    for a in range(4):
        hi, lo = split(own_ref[a])
        both[0 : F * QP, a * E : (a + 1) * E] = hi
        both[F * QP :, a * E : (a + 1) * E] = lo
    k = lax.broadcasted_iota(jnp.int32, (4 * E, E), 0)
    for a in range(4):
        onehot = (k == link_ref[a : a + 1, :]).astype(f32).astype(bf16)
        r = dot(both[...], onehot)
        near_ref[a] = r[0 : F * QP] + r[F * QP :]


def local_kernel(me_ref, state_ref, pred_ref, degree_ref, material_ref, jac_ref, der_ref, base_ref, a_ref, x, s, dscr):
    keep = keep_rows(degree_ref[...], MP)
    for f in range(F):
        x[f] = pad_rows(pred_ref[f], MP) * keep
    a_ref[...] = material_matrix(jac_ref, material_onehot(material_ref[...], me_ref[0]))
    slopes_into(x, load_derivative(der_ref, dscr), s)
    for f in range(F):
        base_ref[f] = pad_rows(state_ref[f], MP)

    def finish(r, lanes, acc):
        for g in range(F):
            base_ref[g, pl.ds(r, 8), lanes] = base_ref[g, pl.ds(r, 8), lanes] - acc[g]

    for half in range(2):
        apply_jacobian(s, a_ref, half, MP // 16, finish)


def flux_kernel(
    me_ref, own_ref, near_ref, base_ref, a_ref, pick_ref, link_ref, normals_ref, trace_ref, lift_ref, degree_ref, material_ref,
    owner_row_ref, owner_col_ref, index_ref, out_ref, u, tscr, far, outside, lscr, dirs, flux,
):
    me = me_ref[0]
    thi, tlo = trace_matrix(trace_ref, tscr)
    for f in range(F):
        phi, plo = split(pick_ref[:, f * 128 : (f + 1) * 128])
        t = dot(thi, phi, NT) + dot(thi, plo, NT) + dot(tlo, phi, NT)
        for a in range(4):
            far[f * QP : (f + 1) * QP, a * 128 : (a + 1) * 128] = t[a * QP : (a + 1) * QP]
    fhi, flo = split(far[...])
    both = jnp.concatenate([fhi, flo], axis=0)
    k = lax.broadcasted_iota(jnp.int32, (4 * 128, E), 0) + 4 * E
    for a in range(4):
        onehot = (k == link_place(link_ref[a : a + 1, :], me)).astype(f32).astype(bf16)
        r = dot(both, onehot)
        outside[a] = near_ref[a] + r[0 : F * QP] + r[F * QP :]
    speed = a_ref[3 * AR : 3 * AR + 1, :] * 0.5
    for a in range(4):
        total = normals_ref[0, a : a + 1, :] * a_ref[0:AR]
        for d in range(1, 3):
            total = total + normals_ref[d, a : a + 1, :] * a_ref[d * AR : (d + 1) * AR]
        dirs[a] = 0.5 * total

    def face(i, carry):
        a, lanes = i // 2, pl.ds(pl.multiple_of((i % 2) * 128, 128), 128)
        sp = a_ref[3 * AR : 3 * AR + 1, lanes] * 0.5
        for f0, f1 in ((0, 5), (5, 9), (9, 13)):
            acc = {}
            for f in range(f0, f1):
                for t in range(4):
                    rows = pl.ds(f * QP + t * 8, 8)
                    acc[f, t] = sp * (own_ref[a, rows, lanes] - outside[a, rows, lanes])
            for g in range(F):
                both_sides = [own_ref[a, pl.ds(g * QP + t * 8, 8), lanes] + outside[a, pl.ds(g * QP + t * 8, 8), lanes] for t in range(4)]
                for f in range(f0, f1):
                    w = jnp.broadcast_to(dirs[a, pl.ds(f * F + g, 1), lanes], (8, 128))
                    for t in range(4):
                        acc[f, t] = acc[f, t] + w * both_sides[t]
            for f in range(f0, f1):
                for t in range(4):
                    flux[f, pl.ds(a * QP + t * 8, 8), lanes] = acc[f, t]
        return carry

    lax.fori_loop(0, 8, face, 0)
    lscr[...] = jnp.zeros(lscr.shape, f32)
    for a in range(4):
        lscr[0:M, a * QP : a * QP + 28] = lift_ref[a]
    lhi, llo = split(lscr[...])
    lhh = jnp.concatenate([lhi, lhi], axis=1)
    keep = keep_rows(degree_ref[...], MS)
    for f in range(F):
        hi, lo = split(flux[f])
        lifted = dot(lhh, jnp.concatenate([hi, lo], axis=0)) + dot(llo, hi)
        u[f * MS : (f + 1) * MS, :] = (base_ref[f, 0:MS, :] - lifted[0:MS]) * keep
    u[INFO : INFO + 8, :] = jnp.concatenate(
        [degree_ref[...], material_ref[...], index_ref[...] + 1, owner_row_ref[...] % 2, jnp.zeros((4, E), jnp.int32)], axis=0
    ).astype(f32)
    owner, other = owner_row_ref[...], owner_col_ref[...]
    rank = ranks(owner, other)
    full = jnp.max(jnp.sum(jnp.where(other // 2 == owner // 2, 1.0, 0.0), axis=0, keepdims=True))
    at = jnp.where(owner % 2 == 0, rank, 5 - rank)
    target, slot = owner // 2 * 2 + at // 3, at % 3
    dest = lax.broadcasted_iota(jnp.int32, (128, E), 0)
    flag = jnp.where(lax.broadcasted_iota(jnp.int32, (128, 384), 1) == INFO + 4 - 768, jnp.where(full > 6.0, 1.0, 0.0), 0.0)
    for c in range(3):
        hi, lo = split(u[c * 384 : (c + 1) * 384, :])
        for j in range(3):
            pick = ((dest == target) & (slot == j)).astype(f32).astype(bf16)
            got = dot(pick, hi, NT) + dot(pick, lo, NT)
            out_ref[:, 0, j * PAY + c * 384 : j * PAY + (c + 1) * 384] = got + flag if c == 2 and j == 0 else got


def ranks(owner_row, owner_col):
    before = lax.broadcasted_iota(jnp.int32, (E, E), 0) < lax.broadcasted_iota(jnp.int32, (E, E), 1)
    return jnp.sum(jnp.where((owner_col == owner_row) & before, 1.0, 0.0), axis=0, keepdims=True).astype(jnp.int32)


def slot_kernel(u_ref, owner_row_ref, owner_col_ref, out_ref):
    slot = owner_row_ref[...] * 4 + ranks(owner_row_ref[...], owner_col_ref[...])
    pick = (lax.broadcasted_iota(jnp.int32, (SLOTS, E), 0) == slot).astype(f32).astype(bf16)
    for c in range(3):
        hi, lo = split(u_ref[c * 384 : (c + 1) * 384, :])
        out_ref[:, c * 384 : (c + 1) * 384] = dot(pick, hi, NT) + dot(pick, lo, NT)


def forward_kernel(core_ref, arrived_ref, out_ref, flag_ref):
    tail = jnp.concatenate([arrived_ref[:, 0, j * PAY + PAY - 128 : (j + 1) * PAY] for j in range(3)], axis=0)
    info = jnp.transpose(tail)
    at = INFO - (PAY - 128)
    foreign = (info[at : at + 1] > 0) & (info[at + 3 : at + 4] != core_ref[0].astype(f32))
    here = jnp.where(foreign, 1.0, 0.0)
    before = lax.broadcasted_iota(jnp.int32, (384, 384), 0) < lax.broadcasted_iota(jnp.int32, (384, 384), 1)
    count = dot(jnp.broadcast_to(here, (16, 384)).astype(bf16), before.astype(f32).astype(bf16))[0:1].astype(jnp.int32)
    place = jnp.where(foreign, count, -1)
    pick = (lax.broadcasted_iota(jnp.int32, (FORWARD, 384), 0) == place).astype(f32).astype(bf16)
    for c in range(3):
        part = [arrived_ref[:, 0, j * PAY + c * 384 : j * PAY + (c + 1) * 384] for j in range(3)]
        hi, lo = split(jnp.concatenate(part, axis=0))
        out_ref[:, c * 384 : (c + 1) * 384] = dot(pick, hi) + dot(pick, lo)
    flag_ref[...] = jnp.broadcast_to(jnp.max(info[at + 4 : at + 5], axis=1, keepdims=True), (1, 128))


def predict_shared_kernel(me_ref, arrived_ref, forwarded_ref, *refs):
    records = jnp.concatenate(
        [arrived_ref[:, 0, j * PAY : (j + 1) * PAY] for j in range(3)] + [forwarded_ref[...], jnp.zeros((SLOTS - 384 - FORWARD, PAY), f32)],
        axis=0,
    )
    predict(me_ref, records, *refs)


def predict_kernel(me_ref, arrived_ref, *refs):
    predict(me_ref, arrived_ref[...], *refs)


def predict(me_ref, arrived, jac_ref, der_ref, corrected_ref, ahead_ref, c, r, x, s, a, dscr, keep, ahead):
    info = jnp.transpose(arrived[:, PAY - 128 :])
    at = INFO - (PAY - 128)
    core = me_ref[1].astype(f32)
    lead = jnp.where(info[at + 3 : at + 4] == core, info[at : at + 1], 0.0)
    slot_row = lax.broadcasted_iota(jnp.int32, (SLOTS, SLOTS), 1)
    slot_col = lax.broadcasted_iota(jnp.int32, (SLOTS, SLOTS), 0)
    degree_col = jnp.where(arrived[:, INFO + 3 : INFO + 4] == core, arrived[:, INFO : INFO + 1], 0.0)
    ahead_of = (degree_col > lead) | ((degree_col == lead) & (slot_col < slot_row))
    rank = jnp.sum(jnp.where(ahead_of, 1.0, 0.0), axis=0, keepdims=True)
    rank = jnp.where(lead > 0, rank, -1.0).astype(jnp.int32)
    pick = (lax.broadcasted_iota(jnp.int32, (E, SLOTS), 0) == rank).astype(f32).astype(bf16)
    for i in range(3):
        hi, lo = split(arrived[:, i * 384 : (i + 1) * 384])
        r[:, i * 384 : (i + 1) * 384] = dot(pick, hi) + dot(pick, lo)
        c[i * 384 : (i + 1) * 384, :] = jnp.transpose(r[:, i * 384 : (i + 1) * 384])
    place = r[:, INFO + 2 : INFO + 3].astype(jnp.int32)
    spread = (lax.broadcasted_iota(jnp.int32, (E, E), 1) + 1 == place).astype(f32).astype(bf16)
    degree = c[INFO : INFO + 1, :].astype(jnp.int32)
    material = c[INFO + 1 : INFO + 2, :].astype(jnp.int32)
    a[...] = material_matrix(jac_ref, material_onehot(material, me_ref[0]))
    keep[...] = keep_rows(degree, MP)
    matrices = load_derivative(der_ref, dscr)
    for f in range(F):
        rows = c[f * MS : (f + 1) * MS, :]
        hi, lo = split(rows)
        corrected_ref[f] = (dot(hi, spread) + dot(lo, spread))[0:M]
        x[f] = pad_rows(rows, MP)
        ahead[f] = time_step * pad_rows(rows, MP)
    top = [jnp.max(degree[:, 128 * half : 128 * (half + 1)]) for half in range(2)]
    blocks = [jnp.where(t <= 2, 1, jnp.where(t == 3, 2, jnp.where(t == 4, 3, jnp.where(t == 5, 4, 6)))) for t in top]

    def step(j, factor):
        factor = factor * time_step / (j + 1).astype(f32)
        slopes_into(x, matrices, s)
        active = jnp.where(degree >= j, factor, 0.0)
        for half in range(2):
            weight = active[:, 128 * half : 128 * (half + 1)]

            def finish(at, lanes, acc):
                kept = -keep[pl.ds(at, 8), lanes]
                for g in range(F):
                    t = acc[g] * kept
                    x[g, pl.ds(at, 8), lanes] = t
                    ahead[g, pl.ds(at, 8), lanes] = ahead[g, pl.ds(at, 8), lanes] + weight * t

            apply_jacobian(s, a, half, jnp.where(j <= top[half], blocks[half], 0), finish)
        return factor

    lax.fori_loop(1, 7, step, jnp.float32(time_step))
    for f in range(F):
        hi, lo = split(ahead[f])
        ahead_ref[f] = (dot(hi, spread) + dot(lo, spread))[0:M]


def call(kernel, outs, scratch, smem, args, flops, limit=24):
    specs = [pl.BlockSpec(memory_space=pltpu.SMEM if i < smem else pltpu.VMEM) for i in range(len(args))]
    return pl.pallas_call(
        kernel,
        out_shape=[jax.ShapeDtypeStruct(o, f32) for o in outs],
        in_specs=specs,
        out_specs=[pl.BlockSpec(memory_space=pltpu.VMEM) for _ in outs],
        scratch_shapes=[pltpu.VMEM(shape, kind) for shape, kind in scratch],
        compiler_params=pltpu.CompilerParams(vmem_limit_bytes=limit * 1024 * 1024),
        cost_estimate=pl.CostEstimate(flops=flops, bytes_accessed=4000000, transcendentals=0),
    )(*args)


def ring(count, step):
    return [(i, (i + step) % count) for i in range(count)]


def shards(
    state, predictor, degree, material, face_link, publish, new_owner, new_index, derivative, trace_ops, lift_ops,
    jacobians, speeds, normals,
):
    core = lax.axis_index("dom").astype(jnp.int32) % 2
    me = jnp.stack([lax.axis_index("narrow").astype(jnp.int32), core])
    row = lambda v: v.reshape(1, E)
    (mine,) = call(pick_kernel, [(8, PICK + JROWS)], [], 0, [predictor, row(degree), publish.reshape(1, 8), jnp.transpose(jacobians, (1, 2, 0, 3)), speeds.reshape(1, 8)], 10**9, 12)
    shared = jnp.concatenate([mine] + [lax.ppermute(mine, "narrow", ring(4, s)) for s in (1, 2, 3)], axis=0)
    picks, jac = shared[:, :PICK], shared[:, PICK:]
    low = lax.ppermute(picks, "dom", ring(128, 1))
    high = lax.ppermute(picks, "dom", ring(128, -1))
    own, near = call(
        trace_kernel,
        [(4, F * QP, E), (4, F * QP, E)],
        [((128, 128), f32), ((2 * F * QP, 4 * E), bf16)],
        0,
        [predictor, row(degree), trace_ops, face_link],
        4 * 10**9,
    )
    base, a = call(
        local_kernel,
        [(F, MP, E), (JROWS, E)],
        [((F, MP, E), f32), ((F, 272, E), f32), ((272, 128), f32)],
        1,
        [me, state, predictor, row(degree), row(material), jac, derivative],
        4 * 10**9,
    )
    around = jnp.concatenate([low, picks, high, jnp.zeros((32, PICK), f32)], axis=0)
    owners = [row(new_owner), new_owner.reshape(E, 1)]
    outgoing, updated = call(
        flux_kernel,
        [(128, 1, 3 * PAY), (PAY, E)],
        [
            ((128, 128), f32),
            ((F * QP, 512), f32),
            ((4, F * QP, E), f32),
            ((96, 128), f32),
            ((4, AR, E), f32),
            ((F, 128, E), f32),
        ],
        1,
        [me, own, near, base, a, around, face_link, normals, trace_ops, lift_ops, row(degree), row(material),
         *owners, row(new_index)],
        4 * 10**9,
    )
    scratch = [
        ((PAY, E), f32),
        ((E, PAY), f32),
        ((F, MP, E), f32),
        ((F, 272, E), f32),
        ((JROWS, E), f32),
        ((272, 128), f32),
        ((MP, E), f32),
        ((F, MP, E), f32),
    ]
    arrived = lax.all_to_all(outgoing, "dom", split_axis=0, concat_axis=0, tiled=True)
    forwarded, flag = call(forward_kernel, [(FORWARD, PAY), (1, 128)], [], 1, [core.reshape(1), arrived], 10**8, 16)
    forwarded = lax.ppermute(forwarded, "dom", [(i, i ^ 1) for i in range(128)])

    def shared(arrived, forwarded, updated, jac, derivative, *rest):
        return tuple(call(
            predict_shared_kernel, [(F, M, E), (F, M, E)], scratch, 1, [me, arrived, forwarded, jac, derivative], 10**10
        ))

    def apart(arrived, forwarded, updated, jac, derivative, *rest):
        (slots,) = call(slot_kernel, [(SLOTS, PAY)], [], 0, [updated, *rest], 10**9)
        slots = lax.all_to_all(slots.reshape(128, 4, PAY), "dom", split_axis=0, concat_axis=0, tiled=True)
        return tuple(call(
            predict_kernel, [(F, M, E), (F, M, E)], scratch, 1, [me, slots.reshape(SLOTS, PAY), jac, derivative], 10**10
        ))

    corrected, ahead = lax.cond(flag[0, 0] > 0, apart, shared, arrived, forwarded, updated, jac, derivative, *owners)
    return corrected, ahead


def solution(mesh):
    both = ("dom", "narrow")
    placed = (
        P(None, None, both), P(None, None, both), P(both), P(both), P(None, both), P(both), P(both), P(both),
        P(), P(), P(), P("narrow", None, None, None), P("narrow"), P(None, None, both),
    )
    return jax.shard_map(
        shards,
        mesh=mesh,
        in_specs=placed,
        out_specs=(P(None, None, both), P(None, None, both)),
        check_vma=False,
    )
```

```python
import functools
import jax
import jax.numpy as jnp
from jax import lax
from jax.experimental import pallas as pl
from jax.experimental.pallas import tpu as pltpu
from jax.sharding import PartitionSpec as P

time_step = 1.5
F = 13
M = 84
MS = 88
MP = 96
E = 256
QP = 32
AR = 176
SLOTS = 512
PAY = 1152
FORWARD = 64
INFO = F * MS
PICK = F * 128
JROWS = 640
f32, bf16 = jnp.float32, jnp.bfloat16


def split(x):
    hi = x.astype(bf16)
    return hi, (x - hi.astype(f32)).astype(bf16)


def dot(a, b, contract=((1,), (0,))):
    return lax.dot_general(a, b, (contract, ((), ())), preferred_element_type=f32)


NT = ((1,), (1,))


def mode_rows(count):
    m = lax.broadcasted_iota(jnp.int32, (count, E), 0)
    deg = jnp.zeros((count, E), jnp.int32)
    for p in range(1, 7):
        deg = deg + (m >= p * (p + 1) * (p + 2) // 6).astype(jnp.int32)
    return jnp.where(m < M, deg, 99)


def keep_rows(degree_row, count):
    return (mode_rows(count) <= degree_row).astype(f32)


def pad_rows(x, rows):
    return jnp.concatenate([x, jnp.zeros((rows - x.shape[0], x.shape[1]), x.dtype)], axis=0)


def load_derivative(der_ref, scr):
    scr[...] = jnp.zeros(scr.shape, f32)
    for d in range(3):
        scr[d * MS : d * MS + M, 0:M] = der_ref[d]
    hi, lo = split(scr[:, 0:M])
    hi, lo = hi.astype(f32), lo.astype(f32)
    return jnp.concatenate([hi, hi, lo], axis=1).astype(bf16)


def slopes_into(x_ref, matrices, s_ref):
    for f in range(F):
        hi, lo = split(x_ref[f, 0:M, :])
        hi, lo = hi.astype(f32), lo.astype(f32)
        s_ref[f] = dot(matrices, jnp.concatenate([hi, lo, hi], axis=0).astype(bf16))


def apply_jacobian(s_ref, a_ref, half, tiles, finish):
    lanes = pl.ds(half * 128, 128)

    def block(r, count):
        acc = [[None] * F for _ in range(count)]
        for d in range(3):
            for f in range(F):
                x = [s_ref[f, pl.ds(d * MS + r + 8 * t, 8), lanes] for t in range(count)]
                for g in range(F):
                    w = jnp.broadcast_to(a_ref[pl.ds(d * AR + g * F + f, 1), lanes], (8, 128))
                    for t in range(count):
                        acc[t][g] = w * x[t] if acc[t][g] is None else acc[t][g] + w * x[t]
        for t in range(count):
            finish(pl.multiple_of(r + 8 * t, 8), lanes, acc[t])

    def body(i, carry):
        block(pl.multiple_of(i * 16, 16), 2)
        return carry

    lax.fori_loop(0, tiles // 2, body, 0)

    @pl.when(tiles % 2 == 1)
    def _():
        block(pl.multiple_of(tiles // 2 * 16, 16), 1)


def material_matrix(jac_ref, onehot):
    table = jac_ref[...]
    hi = table.astype(bf16)
    rest = table - hi.astype(f32)
    mid, lo = split(rest)
    tn = ((0,), (0,))
    return dot(hi, onehot, tn) + dot(mid, onehot, tn) + dot(lo, onehot, tn)


def material_onehot(material_row, me):
    k = lax.broadcasted_iota(jnp.int32, (32, E), 0)
    ident = lax.rem(me - k // 8 + 4, 4) * 8 + k % 8
    return (ident == material_row).astype(f32).astype(bf16)


def pick_kernel(pred_ref, degree_ref, publish_ref, jac_ref, speed_ref, out_ref):
    keep = keep_rows(degree_ref[...], M)
    eye = lax.broadcasted_iota(jnp.int32, (8, 8), 0) == lax.broadcasted_iota(jnp.int32, (8, 8), 1)
    column = lambda v: jnp.sum(jnp.where(eye, v, 0.0), axis=1, keepdims=True)
    published = pad_rows(column(publish_ref[...].astype(f32)), 16).astype(jnp.int32)
    e = lax.broadcasted_iota(jnp.int32, (16, E), 1)
    onehot = (e == published).astype(f32).astype(bf16)
    out_ref[...] = jnp.zeros(out_ref.shape, f32)
    for f in range(F):
        hi, lo = split(pred_ref[f] * keep)
        picked = dot(onehot, hi, NT) + dot(onehot, lo, NT)
        out_ref[:, f * 128 : f * 128 + M] = picked[0:8]
    for d in range(3):
        for g in range(F):
            at = PICK + d * AR + g * F
            out_ref[:, at : at + F] = jac_ref[d, g]
    out_ref[:, PICK + 3 * AR : PICK + 3 * AR + 1] = column(speed_ref[...])


def trace_matrix(trace_ref, scr):
    scr[...] = jnp.zeros(scr.shape, f32)
    for a in range(4):
        scr[a * QP : a * QP + 28, 0:M] = trace_ref[a]
    return split(scr[...])


def link_place(link, me):
    w = link - 4 * E
    block, a, j = w // 32, (w // 8) % 4, w % 8
    step = lax.rem(me - block % 4 + 4, 4)
    far = 4 * E + a * 128 + (block // 4) * 32 + step * 8 + j
    return jnp.where(link < 4 * E, link, far)


def trace_kernel(pred_ref, degree_ref, trace_ref, link_ref, own_ref, near_ref, tscr, both):
    keep = keep_rows(degree_ref[...], MP)
    thi, tlo = trace_matrix(trace_ref, tscr)
    thi, tlo = thi[:, 0:MP], tlo[:, 0:MP]
    thh = jnp.concatenate([thi, thi], axis=1)
    for f in range(F):
        x = pad_rows(pred_ref[f], MP) * keep
        hi, lo = split(x)
        t = dot(thh, jnp.concatenate([hi, lo], axis=0)) + dot(tlo, hi)
        for a in range(4):
            own_ref[a, f * QP : (f + 1) * QP, :] = t[a * QP : (a + 1) * QP]
    for a in range(4):
        hi, lo = split(own_ref[a])
        both[0 : F * QP, a * E : (a + 1) * E] = hi
        both[F * QP :, a * E : (a + 1) * E] = lo
    k = lax.broadcasted_iota(jnp.int32, (4 * E, E), 0)
    for a in range(4):
        onehot = (k == link_ref[a : a + 1, :]).astype(f32).astype(bf16)
        r = dot(both[...], onehot)
        near_ref[a] = r[0 : F * QP] + r[F * QP :]


def local_kernel(me_ref, state_ref, pred_ref, degree_ref, material_ref, jac_ref, der_ref, base_ref, a_ref, x, s, dscr):
    keep = keep_rows(degree_ref[...], MP)
    for f in range(F):
        x[f] = pad_rows(pred_ref[f], MP) * keep
    a_ref[...] = material_matrix(jac_ref, material_onehot(material_ref[...], me_ref[0]))
    slopes_into(x, load_derivative(der_ref, dscr), s)
    for f in range(F):
        base_ref[f] = pad_rows(state_ref[f], MP)

    def finish(r, lanes, acc):
        for g in range(F):
            base_ref[g, pl.ds(r, 8), lanes] = base_ref[g, pl.ds(r, 8), lanes] - acc[g]

    for half in range(2):
        apply_jacobian(s, a_ref, half, MS // 8, finish)


def flux_kernel(
    me_ref, own_ref, near_ref, base_ref, a_ref, pick_ref, link_ref, normals_ref, trace_ref, lift_ref, degree_ref, material_ref,
    owner_row_ref, owner_col_ref, index_ref, out_ref, u, tscr, far, outside, lscr, dirs, flux,
):
    me = me_ref[0]
    thi, tlo = trace_matrix(trace_ref, tscr)
    for f in range(F):
        phi, plo = split(pick_ref[:, f * 128 : (f + 1) * 128])
        t = dot(thi, phi, NT) + dot(thi, plo, NT) + dot(tlo, phi, NT)
        for a in range(4):
            far[f * QP : (f + 1) * QP, a * 128 : (a + 1) * 128] = t[a * QP : (a + 1) * QP]
    fhi, flo = split(far[...])
    both = jnp.concatenate([fhi, flo], axis=0)
    k = lax.broadcasted_iota(jnp.int32, (4 * 128, E), 0) + 4 * E
    for a in range(4):
        onehot = (k == link_place(link_ref[a : a + 1, :], me)).astype(f32).astype(bf16)
        r = dot(both, onehot)
        outside[a] = near_ref[a] + r[0 : F * QP] + r[F * QP :]
    speed = a_ref[3 * AR : 3 * AR + 1, :] * 0.5
    for a in range(4):
        total = normals_ref[0, a : a + 1, :] * a_ref[0:AR]
        for d in range(1, 3):
            total = total + normals_ref[d, a : a + 1, :] * a_ref[d * AR : (d + 1) * AR]
        dirs[a] = 0.5 * total

    def face(i, carry):
        a, lanes = i // 2, pl.ds(pl.multiple_of((i % 2) * 128, 128), 128)
        sp = a_ref[3 * AR : 3 * AR + 1, lanes] * 0.5
        for f0, f1 in ((0, 5), (5, 9), (9, 13)):
            acc = {}
            for f in range(f0, f1):
                for t in range(4):
                    rows = pl.ds(f * QP + t * 8, 8)
                    acc[f, t] = sp * (own_ref[a, rows, lanes] - outside[a, rows, lanes])
            for g in range(F):
                both_sides = [own_ref[a, pl.ds(g * QP + t * 8, 8), lanes] + outside[a, pl.ds(g * QP + t * 8, 8), lanes] for t in range(4)]
                for f in range(f0, f1):
                    w = jnp.broadcast_to(dirs[a, pl.ds(f * F + g, 1), lanes], (8, 128))
                    for t in range(4):
                        acc[f, t] = acc[f, t] + w * both_sides[t]
            for f in range(f0, f1):
                for t in range(4):
                    flux[f, pl.ds(a * QP + t * 8, 8), lanes] = acc[f, t]
        return carry

    lax.fori_loop(0, 8, face, 0)
    lscr[...] = jnp.zeros(lscr.shape, f32)
    for a in range(4):
        lscr[0:M, a * QP : a * QP + 28] = lift_ref[a]
    lhi, llo = split(lscr[...])
    lhh = jnp.concatenate([lhi, lhi], axis=1)
    keep = keep_rows(degree_ref[...], MS)
    for f in range(F):
        hi, lo = split(flux[f])
        lifted = dot(lhh, jnp.concatenate([hi, lo], axis=0)) + dot(llo, hi)
        u[f * MS : (f + 1) * MS, :] = (base_ref[f, 0:MS, :] - lifted[0:MS]) * keep
    u[INFO : INFO + 8, :] = jnp.concatenate(
        [degree_ref[...], material_ref[...], index_ref[...] + 1, owner_row_ref[...] % 2, jnp.zeros((4, E), jnp.int32)], axis=0
    ).astype(f32)
    owner, other = owner_row_ref[...], owner_col_ref[...]
    rank = ranks(owner, other)
    full = jnp.max(jnp.sum(jnp.where(other // 2 == owner // 2, 1.0, 0.0), axis=0, keepdims=True))
    at = jnp.where(owner % 2 == 0, rank, 5 - rank)
    target, slot = owner // 2 * 2 + at // 3, at % 3
    dest = lax.broadcasted_iota(jnp.int32, (128, E), 0)
    flag = jnp.where(lax.broadcasted_iota(jnp.int32, (128, 384), 1) == INFO + 4 - 768, jnp.where(full > 6.0, 1.0, 0.0), 0.0)
    for c in range(3):
        hi, lo = split(u[c * 384 : (c + 1) * 384, :])
        for j in range(3):
            pick = ((dest == target) & (slot == j)).astype(f32).astype(bf16)
            got = dot(pick, hi, NT) + dot(pick, lo, NT)
            out_ref[:, 0, j * PAY + c * 384 : j * PAY + (c + 1) * 384] = got + flag if c == 2 and j == 0 else got


def ranks(owner_row, owner_col):
    before = lax.broadcasted_iota(jnp.int32, (E, E), 0) < lax.broadcasted_iota(jnp.int32, (E, E), 1)
    return jnp.sum(jnp.where((owner_col == owner_row) & before, 1.0, 0.0), axis=0, keepdims=True).astype(jnp.int32)


def slot_kernel(u_ref, owner_row_ref, owner_col_ref, out_ref):
    slot = owner_row_ref[...] * 4 + ranks(owner_row_ref[...], owner_col_ref[...])
    pick = (lax.broadcasted_iota(jnp.int32, (SLOTS, E), 0) == slot).astype(f32).astype(bf16)
    for c in range(3):
        hi, lo = split(u_ref[c * 384 : (c + 1) * 384, :])
        out_ref[:, c * 384 : (c + 1) * 384] = dot(pick, hi, NT) + dot(pick, lo, NT)


def forward_kernel(core_ref, arrived_ref, out_ref, flag_ref):
    tail = jnp.concatenate([arrived_ref[:, 0, j * PAY + PAY - 128 : (j + 1) * PAY] for j in range(3)], axis=0)
    info = jnp.transpose(tail)
    at = INFO - (PAY - 128)
    foreign = (info[at : at + 1] > 0) & (info[at + 3 : at + 4] != core_ref[0].astype(f32))
    here = jnp.where(foreign, 1.0, 0.0)
    before = lax.broadcasted_iota(jnp.int32, (384, 384), 0) < lax.broadcasted_iota(jnp.int32, (384, 384), 1)
    count = dot(jnp.broadcast_to(here, (16, 384)).astype(bf16), before.astype(f32).astype(bf16))[0:1].astype(jnp.int32)
    place = jnp.where(foreign, count, -1)
    pick = (lax.broadcasted_iota(jnp.int32, (FORWARD, 384), 0) == place).astype(f32).astype(bf16)
    for c in range(3):
        part = [arrived_ref[:, 0, j * PAY + c * 384 : j * PAY + (c + 1) * 384] for j in range(3)]
        hi, lo = split(jnp.concatenate(part, axis=0))
        out_ref[:, c * 384 : (c + 1) * 384] = dot(pick, hi) + dot(pick, lo)
    flag_ref[...] = jnp.broadcast_to(jnp.max(info[at + 4 : at + 5], axis=1, keepdims=True), (1, 128))


def predict_shared_kernel(me_ref, arrived_ref, forwarded_ref, *refs):
    records = jnp.concatenate(
        [arrived_ref[:, 0, j * PAY : (j + 1) * PAY] for j in range(3)] + [forwarded_ref[...], jnp.zeros((SLOTS - 384 - FORWARD, PAY), f32)],
        axis=0,
    )
    predict(me_ref, records, *refs)


def predict_kernel(me_ref, arrived_ref, *refs):
    predict(me_ref, arrived_ref[...], *refs)


def predict(me_ref, arrived, jac_ref, der_ref, corrected_ref, ahead_ref, c, r, x, s, a, dscr, keep, ahead):
    info = jnp.transpose(arrived[:, PAY - 128 :])
    at = INFO - (PAY - 128)
    core = me_ref[1].astype(f32)
    lead = jnp.where(info[at + 3 : at + 4] == core, info[at : at + 1], 0.0)
    slot_row = lax.broadcasted_iota(jnp.int32, (SLOTS, SLOTS), 1)
    slot_col = lax.broadcasted_iota(jnp.int32, (SLOTS, SLOTS), 0)
    degree_col = jnp.where(arrived[:, INFO + 3 : INFO + 4] == core, arrived[:, INFO : INFO + 1], 0.0)
    ahead_of = (degree_col > lead) | ((degree_col == lead) & (slot_col < slot_row))
    rank = jnp.sum(jnp.where(ahead_of, 1.0, 0.0), axis=0, keepdims=True)
    rank = jnp.where(lead > 0, rank, -1.0).astype(jnp.int32)
    pick = (lax.broadcasted_iota(jnp.int32, (E, SLOTS), 0) == rank).astype(f32).astype(bf16)
    for i in range(3):
        hi, lo = split(arrived[:, i * 384 : (i + 1) * 384])
        r[:, i * 384 : (i + 1) * 384] = dot(pick, hi) + dot(pick, lo)
        c[i * 384 : (i + 1) * 384, :] = jnp.transpose(r[:, i * 384 : (i + 1) * 384])
    place = r[:, INFO + 2 : INFO + 3].astype(jnp.int32)
    spread = (lax.broadcasted_iota(jnp.int32, (E, E), 1) + 1 == place).astype(f32).astype(bf16)
    degree = c[INFO : INFO + 1, :].astype(jnp.int32)
    material = c[INFO + 1 : INFO + 2, :].astype(jnp.int32)
    a[...] = material_matrix(jac_ref, material_onehot(material, me_ref[0]))
    keep[...] = keep_rows(degree, MP)
    matrices = load_derivative(der_ref, dscr)
    for f in range(F):
        rows = c[f * MS : (f + 1) * MS, :]
        hi, lo = split(rows)
        corrected_ref[f] = (dot(hi, spread) + dot(lo, spread))[0:M]
        x[f] = pad_rows(rows, MP)
        ahead[f] = time_step * pad_rows(rows, MP)
    top = [jnp.max(degree[:, 128 * half : 128 * (half + 1)]) for half in range(2)]
    tiles = [jnp.where(t <= 2, 2, jnp.where(t == 3, 3, jnp.where(t == 4, 5, jnp.where(t == 5, 7, 11)))) for t in top]

    def step(j, factor):
        factor = factor * time_step / (j + 1).astype(f32)
        slopes_into(x, matrices, s)
        active = jnp.where(degree >= j, factor, 0.0)
        for half in range(2):
            weight = active[:, 128 * half : 128 * (half + 1)]

            def finish(at, lanes, acc):
                kept = -keep[pl.ds(at, 8), lanes]
                for g in range(F):
                    t = acc[g] * kept
                    x[g, pl.ds(at, 8), lanes] = t
                    ahead[g, pl.ds(at, 8), lanes] = ahead[g, pl.ds(at, 8), lanes] + weight * t

            apply_jacobian(s, a, half, jnp.where(j <= top[half], tiles[half], 0), finish)
        return factor

    lax.fori_loop(1, 7, step, jnp.float32(time_step))
    for f in range(F):
        hi, lo = split(ahead[f])
        ahead_ref[f] = (dot(hi, spread) + dot(lo, spread))[0:M]


def call(kernel, outs, scratch, smem, args, flops, limit=24):
    specs = [pl.BlockSpec(memory_space=pltpu.SMEM if i < smem else pltpu.VMEM) for i in range(len(args))]
    return pl.pallas_call(
        kernel,
        out_shape=[jax.ShapeDtypeStruct(o, f32) for o in outs],
        in_specs=specs,
        out_specs=[pl.BlockSpec(memory_space=pltpu.VMEM) for _ in outs],
        scratch_shapes=[pltpu.VMEM(shape, kind) for shape, kind in scratch],
        compiler_params=pltpu.CompilerParams(vmem_limit_bytes=limit * 1024 * 1024),
        cost_estimate=pl.CostEstimate(flops=flops, bytes_accessed=4000000, transcendentals=0),
    )(*args)


def ring(count, step):
    return [(i, (i + step) % count) for i in range(count)]


def shards(
    state, predictor, degree, material, face_link, publish, new_owner, new_index, derivative, trace_ops, lift_ops,
    jacobians, speeds, normals,
):
    core = lax.axis_index("dom").astype(jnp.int32) % 2
    me = jnp.stack([lax.axis_index("narrow").astype(jnp.int32), core])
    row = lambda v: v.reshape(1, E)
    (mine,) = call(pick_kernel, [(8, PICK + JROWS)], [], 0, [predictor, row(degree), publish.reshape(1, 8), jnp.transpose(jacobians, (1, 2, 0, 3)), speeds.reshape(1, 8)], 10**9, 60)
    shared = jnp.concatenate([mine] + [lax.ppermute(mine, "narrow", ring(4, s)) for s in (1, 2, 3)], axis=0)
    picks, jac = shared[:, :PICK], shared[:, PICK:]
    low = lax.ppermute(picks, "dom", ring(128, 1))
    high = lax.ppermute(picks, "dom", ring(128, -1))
    own, near = call(
        trace_kernel,
        [(4, F * QP, E), (4, F * QP, E)],
        [((128, 128), f32), ((2 * F * QP, 4 * E), bf16)],
        0,
        [predictor, row(degree), trace_ops, face_link],
        4 * 10**9,
    )
    base, a = call(
        local_kernel,
        [(F, MP, E), (JROWS, E)],
        [((F, MP, E), f32), ((F, 272, E), f32), ((272, 128), f32)],
        1,
        [me, state, predictor, row(degree), row(material), jac, derivative],
        4 * 10**9,
    )
    around = jnp.concatenate([low, picks, high, jnp.zeros((32, PICK), f32)], axis=0)
    owners = [row(new_owner), new_owner.reshape(E, 1)]
    outgoing, updated = call(
        flux_kernel,
        [(128, 1, 3 * PAY), (PAY, E)],
        [
            ((128, 128), f32),
            ((F * QP, 512), f32),
            ((4, F * QP, E), f32),
            ((96, 128), f32),
            ((4, AR, E), f32),
            ((F, 128, E), f32),
        ],
        1,
        [me, own, near, base, a, around, face_link, normals, trace_ops, lift_ops, row(degree), row(material),
         *owners, row(new_index)],
        4 * 10**9,
    )
    scratch = [
        ((PAY, E), f32),
        ((E, PAY), f32),
        ((F, MP, E), f32),
        ((F, 272, E), f32),
        ((JROWS, E), f32),
        ((272, 128), f32),
        ((MP, E), f32),
        ((F, MP, E), f32),
    ]
    arrived = lax.all_to_all(outgoing, "dom", split_axis=0, concat_axis=0, tiled=True)
    forwarded, flag = call(forward_kernel, [(FORWARD, PAY), (1, 128)], [], 1, [core.reshape(1), arrived], 10**8, 16)
    forwarded = lax.ppermute(forwarded, "dom", [(i, i ^ 1) for i in range(128)])

    def shared(arrived, forwarded, updated, jac, derivative, *rest):
        return tuple(call(
            predict_shared_kernel, [(F, M, E), (F, M, E)], scratch, 1, [me, arrived, forwarded, jac, derivative], 10**10
        ))

    def apart(arrived, forwarded, updated, jac, derivative, *rest):
        (slots,) = call(slot_kernel, [(SLOTS, PAY)], [], 0, [updated, *rest], 10**9)
        slots = lax.all_to_all(slots.reshape(128, 4, PAY), "dom", split_axis=0, concat_axis=0, tiled=True)
        return tuple(call(
            predict_kernel, [(F, M, E), (F, M, E)], scratch, 1, [me, slots.reshape(SLOTS, PAY), jac, derivative], 10**10
        ))

    corrected, ahead = lax.cond(flag[0, 0] > 0, apart, shared, arrived, forwarded, updated, jac, derivative, *owners)
    return corrected, ahead


def solution(mesh):
    both = ("dom", "narrow")
    placed = (
        P(None, None, both), P(None, None, both), P(both), P(both), P(None, both), P(both), P(both), P(both),
        P(), P(), P(), P("narrow", None, None, None), P("narrow"), P(None, None, both),
    )
    return jax.shard_map(
        shards,
        mesh=mesh,
        in_specs=placed,
        out_specs=(P(None, None, both), P(None, None, both)),
        check_vma=False,
    )
```
